128 devices in a mesh: lag: 4 (over y_hi, core), row: 32 (over y_lo, z, x).
Axes of the slice: x: 4, y: 4 (y_hi: 2, y_lo: 2; y = y_hi * 2 + y_lo), z: 4, core: 2. Of those that a mesh axis runs over, the one named last changes fastest.
Arguments:
- history: bfloat16 [64, 16, 16384], P('lag'), may hold values from -6 to 6
- tiles: bfloat16 [64, 128, 8, 128, 128], P('lag', 'row'), may hold values from -0.015625 to 0.015625
- columns: int32 [64, 128, 8], P('lag', 'row'), may hold values from 0 to 127
- counts: int32 [64, 128], P('lag', 'row'), may hold values from 1 to 8, as said below
- inverse: bfloat16 [128, 128, 128], P('row')
- excitation: float32 [16, 16, 16384], P(None, None, 'row'), may hold values from -6 to 6
Outputs:
- solutions: bfloat16 [16, 16, 16384], P(None, None, 'row')
The draws below stay inside these ranges and needn't reach their ends.
Inputs may be any that keep to these rules, and one draw needn't show every extreme that they name: Slots 0 .. counts - 1 of a row block hold its tiles, the rest are padding; in every lag some row block fills all 8 slots.
All inputs are finite; a program needn't handle non-finite values.
Results may differ from the reference program's by a relative error of at most 0.0051.
Values may be sent and summed in bfloat16 or wider, within the bound.
A program may use at most 128 MiB of HBM per device.

```python
import jax
import jax.numpy as jnp
from jax import lax

PULSES = 16
TILE = 128
LAGS = 64
KSLOTS = 8
STEPS = 16
NRB = 128
UNKNOWNS = 16384


def draw_counts(key, part):
    key = jax.random.fold_in(key, 11)
    first = jax.random.fold_in(key, 1)
    second = jax.random.fold_in(key, 2)
    base = jax.random.randint(first, (LAGS, NRB), 1, KSLOTS + 1)
    filled = jax.random.randint(second, (LAGS,), 0, NRB)
    where_full = jnp.arange(NRB)[None, :] == filled[:, None]
    return jnp.where(where_full, KSLOTS, base).astype(jnp.int32)


def draw_inverse(key, part):
    key = jax.random.fold_in(key, 23)
    first = jax.random.fold_in(key, 1)
    second = jax.random.fold_in(key, 2)
    diag_values = jax.random.uniform(first, (NRB, TILE), jnp.float32, 0.6, 1.6)
    spread = jax.random.normal(second, (NRB, TILE, TILE), jnp.float32)
    eye = jnp.eye(TILE, dtype=jnp.float32)[None]
    matrix = eye * diag_values[:, :, None] + spread * (0.25 / TILE ** 0.5)
    return matrix.astype(jnp.bfloat16)


def touch_ends(array, key, low, high):
    dims = array.shape
    place = [jax.random.randint(jax.random.fold_in(key, axis), (), 0, dims[axis]) for axis in range(len(dims))]
    array = array.at[tuple(place)].set(low)
    longest = dims.index(max(dims))
    place[longest] = (place[longest] + 1) % dims[longest]
    return array.at[tuple(place)].set(high)


def block_levels(own_key, dims, shards, smallest, high):
    def one(dim, parts):
        draws = jax.random.uniform(jax.random.fold_in(jax.random.fold_in(own_key, 6), dim), (parts,), jnp.float32, smallest / len(shards), high / len(shards))
        return jnp.repeat(jnp.exp(draws), dims[dim] // parts).reshape((-1,) + (1,) * (len(dims) - dim - 1))

    factor_of = one(*shards[0])
    for cut in shards[1:]:
        factor_of = factor_of * one(*cut)
    return factor_of


def bell_draw(own_key, shape, width, reach, cuts=(), held_as=jnp.bfloat16):
    entries = width * jax.random.normal(own_key, shape, jnp.float32)
    if cuts:
        entries = entries * block_levels(own_key, shape, cuts, -0.22, 0.18)
    return jnp.clip(entries, -reach, reach).astype(held_as)


def setup_inputs(seed: int = 0) -> dict:
    key_of = jax.random.split(jax.random.key(seed), 7)
    return {
        "history": bell_draw(key_of[0], (LAGS, PULSES, UNKNOWNS), 1.0, 6.0, ((0, 4),)),
        "tiles": bell_draw(key_of[1], (LAGS, NRB, KSLOTS, TILE, TILE), (2 * LAGS * KSLOTS * TILE) ** -0.5, 0.015625, ((0, 4), (1, 32))),
        "columns": touch_ends(jax.random.randint(key_of[2], (LAGS, NRB, KSLOTS), 0, NRB), jax.random.fold_in(key_of[2], 1), 0, NRB - 1).astype(jnp.int32),
        "counts": draw_counts(jax.random.fold_in(key_of[6], 71), 0),
        "inverse": draw_inverse(jax.random.fold_in(key_of[6], 71), 0),
        "excitation": bell_draw(key_of[5], (STEPS, PULSES, UNKNOWNS), 1.0, 6.0, ((2, 32),), jnp.float32),
    }


def reference(history, tiles, columns, counts, inverse, excitation):
    keep = (jnp.arange(KSLOTS)[None, None, :] < counts[:, :, None]).astype(jnp.bfloat16)
    current = history
    results = []
    for step in range(STEPS):
        def one_lag(total, items):
            tile_lag, column_lag, keep_lag, hist_lag = items
            blocks = hist_lag.reshape(PULSES, NRB, TILE)
            picked = blocks[:, column_lag, :] * keep_lag[None, :, :, None]
            term = jnp.einsum('bkic,pbkc->pbi', tile_lag.astype(jnp.float32), picked.astype(jnp.float32))
            return total + term, None

        start = jnp.zeros((PULSES, NRB, TILE), jnp.float32)
        scattered, unused = lax.scan(one_lag, start, (tiles, columns, keep, current))
        field = excitation[step] - scattered.reshape(PULSES, UNKNOWNS)
        rhs = field.astype(jnp.bfloat16).reshape(PULSES, NRB, TILE)
        solved = jnp.einsum('bij,pbj->pbi', inverse.astype(jnp.float32), rhs.astype(jnp.float32))
        solved = solved.astype(jnp.bfloat16).reshape(PULSES, UNKNOWNS)
        results.append(solved)
        current = jnp.concatenate([solved[None], current[:-1]], axis=0)
    return jnp.stack(results)
```

```python
import jax
import jax.numpy as jnp
from jax import lax
from jax.experimental import pallas as pl
from jax.experimental.pallas import tpu as pltpu
from jax.sharding import PartitionSpec as P

MESH = pl.DeviceIdType.MESH
LAG_AXIS, ROW_AXIS = "lag", "row"
NY, NZ, NX = 2, 4, 4
ROWS = NY * NZ * NX
GROUPS = 4
LAGS = 16
RB = 4
KS = 8
T = 128
PULSES = 16
HALF = 8
STEPS = 16
SENT = STEPS - 1
NB = 128
WIDTH = RB * T
NEAR = 8


def ring_hops(d, n):
    return min(d, n - d)


OFFSETS = sorted(
    [(a, b, c) for a in range(NY) for b in range(NZ) for c in range(NX)][1:],
    key=lambda o: -(o[0] + ring_hops(o[1], NZ) + ring_hops(o[2], NX)),
)


def dot_t(a, b):
    return lax.dot_general(a, b, (((1,), (1,)), ((), ())), preferred_element_type=jnp.float32)


def kernel(
    columns, counts, hist_hbm, tiles_hbm, inv_hbm, exc_hbm, out_ref,
    tiles, h0, land, work, inv, exc, acc, base, part, parts, solf, outbuf,
    tsem, hsem, isem, esem, recv_a, recv_b, send_a, send_b,
    hrecv, slice_recv, slice_send, fwd_send, stream_send, part_send, part_recv, out_send, out_recv,
):
    g = lax.axis_index(LAG_AXIS)
    r = lax.axis_index(ROW_AXIS)
    y, z, x = r // (NZ * NX), (r // NX) % NZ, r % NX
    partner = (NY - 1 - y) * (NZ * NX) + z * NX + x

    def peer(o):
        return ((y + o[0]) % NY) * (NZ * NX) + ((z + o[1]) % NZ) * NX + (x + o[2]) % NX

    for l in range(LAGS):
        pltpu.make_async_copy(tiles_hbm.at[l], tiles.at[l], tsem.at[l]).start()

    def load_block(c, carry):
        pltpu.make_async_copy(
            hist_hbm.at[:, :, pl.ds(pl.multiple_of(c * T, T), T)], h0.at[:, c], hsem
        ).start()
        return carry

    lax.fori_loop(0, NB, load_block, 0)
    inv_copy = pltpu.make_async_copy(inv_hbm, inv, isem)
    inv_copy.start()
    exc_copy = pltpu.make_async_copy(exc_hbm, exc, esem)
    exc_copy.start()

    barrier = pltpu.get_barrier_semaphore()

    def greet(lag, row):
        pl.semaphore_signal(barrier, inc=1, device_id=(lag, row), device_id_type=MESH)

    @pl.when(g % 2 == 0)
    def _():
        for o in OFFSETS:
            greet(g, peer(o))

    @pl.when(g == 0)
    def _():
        for other in (1, 2, 3):
            greet(other, r)
        pl.semaphore_wait(barrier, ROWS - 1 + 3)

    @pl.when(g == 1)
    def _():
        greet(0, r)
        greet(2, partner)
        pl.semaphore_wait(barrier, 2)

    @pl.when(g == 2)
    def _():
        greet(0, r)
        greet(3, r)
        greet(1, partner)
        pl.semaphore_wait(barrier, ROWS - 1 + 3)

    @pl.when(g == 3)
    def _():
        greet(0, r)
        greet(2, r)
        pl.semaphore_wait(barrier, 2)

    def slice_copy(tau, i):
        c = RB * partner + i
        return pltpu.make_async_remote_copy(
            hist_hbm.at[LAGS - 1 - tau, :, pl.ds(pl.multiple_of(c * T, T), T)],
            land.at[tau, c],
            slice_send.at[tau],
            slice_recv.at[tau],
            device_id=(2, partner),
            device_id_type=MESH,
        )

    @pl.when(g == 1)
    def _():
        def one(tau, carry):
            for i in range(RB):
                slice_copy(tau, i).start()
            return carry

        lax.fori_loop(0, SENT, one, 0)

    zero_block = jnp.zeros((T // 8, T), jnp.bfloat16)
    acc[...] = jnp.zeros_like(acc)
    for e in range(LAGS):
        h0[e, NB] = zero_block
    for tau in range(SENT):
        work[tau, 0, NB] = zero_block
        work[tau, 1, NB] = zero_block

    pltpu.make_async_copy(h0.at[:, pl.ds(0, NB)], h0.at[:, pl.ds(0, NB)], hsem).wait()

    def stream_copy(tau):
        return pltpu.make_async_remote_copy(
            h0.at[LAGS - 1 - tau, pl.ds(0, NB)],
            land.at[tau],
            stream_send.at[tau],
            hrecv.at[tau],
            device_id=(g + 1, r),
            device_id_type=MESH,
        )

    @pl.when(g % 2 == 0)
    def _():
        def one(tau, carry):
            stream_copy(tau).start()
            return carry

        lax.fori_loop(0, SENT, one, 0)

    def column(l, b, k):
        return jnp.where(k < counts[l, b], columns[l, b, k], NB)

    def weights(l, b):
        return jnp.concatenate([tiles[l, b, k] for k in range(KS)], axis=1)

    for quarter in range(4):
        entries = 4 * quarter + 4

        def own_lag(l, carry):
            pltpu.make_async_copy(tiles.at[l], tiles.at[l], tsem.at[l]).wait()
            for b in range(RB):
                xs = [
                    h0[0:entries, column(l, b, k)].reshape(entries * PULSES, T) for k in range(KS)
                ]
                got = dot_t(jnp.concatenate(xs, axis=1), weights(l, b))
                here = (pl.ds(LAGS - 1 - l, entries), slice(None), pl.ds(b * T, T))
                acc[here] += got.reshape(entries, PULSES, T)
            return carry

        lax.fori_loop(4 * quarter, 4 * quarter + 4, own_lag, 0)

    inv_copy.wait()
    exc_copy.wait()

    def part_copy(s, ch):
        return pltpu.make_async_remote_copy(
            part.at[s, ch],
            parts.at[s, ch, g - 1],
            part_send.at[s],
            part_recv.at[s],
            device_id=(0, r),
            device_id_type=MESH,
        )

    def send_part(s):
        for ch in range(2):
            part[s, ch] = acc[STEPS - 1 - s, pl.ds(ch * HALF, HALF), :]
        for ch in range(2):
            part_copy(s, ch).start()

    def forward_copy(tau, o):
        here = land.at[tau, pl.ds(RB * r, RB)]
        return pltpu.make_async_remote_copy(
            here, here, fwd_send.at[tau], hrecv.at[tau], device_id=(2, peer(o)), device_id_type=MESH
        )

    def forward(tau):
        here = land.at[tau, pl.ds(RB * r, RB)]
        pltpu.make_async_copy(here, here, slice_recv.at[tau]).wait()
        for o in OFFSETS:
            forward_copy(tau, o).start()

    @pl.when(g > 0)
    def _():
        send_part(0)

        @pl.when(g == 2)
        def _():
            def one(tau, carry):
                forward(tau)
                return carry

            lax.fori_loop(0, 2, one, 0)

        def entry(tau, carry):
            @pl.when((g == 2) & (tau < SENT - 2))
            def _():
                forward(tau + 2)

            @pl.when(g == 2)
            def _():
                arrived = land.at[tau, pl.ds(0, NB - RB)]
                pltpu.make_async_copy(arrived, arrived, hrecv.at[tau]).wait()

            @pl.when(g != 2)
            def _():
                pltpu.make_async_copy(land.at[tau], land.at[tau], hrecv.at[tau]).wait()

            work[tau, 0, pl.ds(0, NB)] = land[tau]

            def push(lag, carry):
                for b in range(RB):
                    xs = [work[tau, 0, column(lag - 1, b, k)] for k in range(KS)]
                    got = dot_t(jnp.concatenate(xs, axis=1), weights(lag - 1, b))
                    here = (STEPS - 1 - (tau + lag), slice(None), pl.ds(b * T, T))
                    acc[here] += got
                return carry

            lax.fori_loop(1, STEPS - tau, push, 0)
            send_part(tau + 1)
            return carry

        lax.fori_loop(0, SENT, entry, 0)

    low = lax.broadcasted_iota(jnp.int32, (2 * HALF, T), 0) < HALF
    keep_low = jnp.where(low, 1.0, 0.0).astype(jnp.bfloat16)
    keep_high = jnp.where(low, 0.0, 1.0).astype(jnp.bfloat16)
    recv = (recv_a, recv_b)
    send = (send_a, send_b)

    def own_slot(s, ch):
        return land.at[s, pl.ds(ch * (NB // 2) + 2 * r, 2)]

    def solution_copy(s, ch, o):
        here = own_slot(s, ch)
        return pltpu.make_async_remote_copy(
            here, here, send[ch].at[s], recv[ch].at[s], device_id=(0, peer(o)), device_id_type=MESH
        )

    def out_copy(s, other):
        return pltpu.make_async_remote_copy(
            outbuf.at[s], outbuf.at[s], out_send.at[s], out_recv, device_id=(other, r), device_id_type=MESH
        )

    def folded(got):
        return got[0:HALF] + got[HALF : 2 * HALF]

    def set_base(s):
        pltpu.make_async_copy(parts.at[s], parts.at[s], part_recv.at[s]).wait()
        for ch in range(2):
            rows = pl.ds(ch * HALF, HALF)
            other = parts[s, ch, 0] + parts[s, ch, 1] + parts[s, ch, 2]
            base[ch] = exc[s, rows, :] - (acc[STEPS - 1 - s, rows, :] + other)

    def chain(s, ch, first):
        if not first:
            tau = s - 1
            arrived = land.at[tau, pl.ds(0, NB // 2 - 2)]
            pltpu.make_async_copy(arrived, arrived, recv[ch].at[tau]).wait()
            pairs = land[tau, pl.ds(ch * (NB // 2), NB // 2)]
            split = jnp.stack([pairs * keep_low, pairs * keep_high], axis=1)
            work[tau, ch, pl.ds(0, NB)] = split.reshape(NB, 2 * HALF, T)
        solved = []
        for b in range(RB):
            cols = pl.ds(b * T, T)
            field = base[ch, :, cols]
            if not first:
                xs = [work[tau, ch, column(0, b, k)] for k in range(KS)]
                field = field - folded(dot_t(jnp.concatenate(xs, axis=1), weights(0, b)))
            solved.append(dot_t(field.astype(jnp.bfloat16), inv[b]))
        for b in range(RB):
            solf[pl.ds(ch * HALF, HALF), pl.ds(b * T, T)] = solved[b]

        def publish():
            for i in range(2):
                pair = jnp.concatenate([solved[2 * i], solved[2 * i + 1]], axis=0)
                land[s, ch * (NB // 2) + 2 * r + i] = pair.astype(jnp.bfloat16)
            for o in OFFSETS:
                solution_copy(s, ch, o).start()

        if first:
            publish()
        else:
            pl.when(s < SENT)(publish)

    def hand_out(s):
        outbuf[s] = solf[...].astype(jnp.bfloat16)
        for other in (1, 2, 3):
            out_copy(s, other).start()

    def later(s):
        near = jnp.minimum(s, NEAR - 1)
        far = jnp.maximum(NEAR - s, 0)

        def one(n, carry):
            is_near = n < near
            lag = jnp.where(is_near, n + 2, n - near + NEAR + 1)
            tau = jnp.where(is_near, s + 1 - lag, s - 1)
            target = tau + lag
            for b in range(RB):
                cs = [column(lag - 1, b, k) for k in range(KS)]
                xa = jnp.concatenate([work[tau, 0, c] for c in cs], axis=1)
                xb = jnp.concatenate([work[tau, 1, c] for c in cs], axis=1)
                got = dot_t(jnp.concatenate([xa, xb], axis=0), weights(lag - 1, b))
                here = (STEPS - 1 - target, slice(None), pl.ds(b * T, T))
                acc[here] += jnp.concatenate(
                    [folded(got[0 : 2 * HALF]), folded(got[2 * HALF : 4 * HALF])], axis=0
                )
            return carry

        lax.fori_loop(0, near + far, one, 0)

    @pl.when(g == 0)
    def _():
        set_base(0)
        chain(0, 0, True)
        chain(0, 1, True)
        hand_out(0)
        set_base(1)

        def step(s, carry):
            chain(s, 0, False)
            chain(s, 1, False)
            hand_out(s)

            @pl.when(s < STEPS - 1)
            def _():
                later(s)
                set_base(s + 1)

            return carry

        lax.fori_loop(1, STEPS, step, 0)

        def drain(s, carry):
            sent = land.at[s, pl.ds(0, NB // 2 - 2)]
            for ch in range(2):
                pltpu.make_async_copy(sent, sent, send[ch].at[s]).wait()
            return carry

        lax.fori_loop(0, SENT, drain, 0)

        def drain_out(s, carry):
            for other in (1, 2, 3):
                out_copy(s, other).wait_send()
            return carry

        lax.fori_loop(0, STEPS, drain_out, 0)

    @pl.when(g > 0)
    def _():
        pltpu.make_async_copy(outbuf, outbuf, out_recv).wait()

        def drain(s, carry):
            pltpu.make_async_copy(part.at[s], part.at[s], part_send.at[s]).wait()
            return carry

        lax.fori_loop(0, STEPS, drain, 0)

    @pl.when(g % 2 == 0)
    def _():
        def drain(tau, carry):
            stream_copy(tau).wait_send()
            return carry

        lax.fori_loop(0, SENT, drain, 0)

    @pl.when(g == 1)
    def _():
        def drain(tau, carry):
            sent = land.at[tau, pl.ds(0, RB)]
            pltpu.make_async_copy(sent, sent, slice_send.at[tau]).wait()
            return carry

        lax.fori_loop(0, SENT, drain, 0)

    @pl.when(g == 2)
    def _():
        def drain(tau, carry):
            sent = land.at[tau, pl.ds(0, NB - RB)]
            pltpu.make_async_copy(sent, sent, fwd_send.at[tau]).wait()
            return carry

        lax.fori_loop(0, SENT, drain, 0)

    out_ref[...] = outbuf[...]


def local(history, tiles, columns, counts, inverse, excitation):
    smem = pl.BlockSpec(memory_space=pltpu.SMEM)
    hbm = pl.BlockSpec(memory_space=pl.ANY)
    dma = pltpu.SemaphoreType.DMA
    bf16, f32 = jnp.bfloat16, jnp.float32
    return pl.pallas_call(
        kernel,
        out_shape=jax.ShapeDtypeStruct((STEPS, PULSES, WIDTH), bf16),
        in_specs=[smem, smem, hbm, hbm, hbm, hbm],
        out_specs=pl.BlockSpec(memory_space=pltpu.VMEM),
        scratch_shapes=[
            pltpu.VMEM((LAGS, RB, KS, T, T), bf16),
            pltpu.VMEM((LAGS, NB + 1, PULSES, T), bf16),
            pltpu.VMEM((SENT, NB, PULSES, T), bf16),
            pltpu.VMEM((SENT, 2, NB + 1, PULSES, T), bf16),
            pltpu.VMEM((RB, T, T), bf16),
            pltpu.VMEM((STEPS, PULSES, WIDTH), f32),
            pltpu.VMEM((STEPS + 3, PULSES, WIDTH), f32),
            pltpu.VMEM((2, HALF, WIDTH), f32),
            pltpu.VMEM((STEPS, 2, HALF, WIDTH), f32),
            pltpu.VMEM((STEPS, 2, 3, HALF, WIDTH), f32),
            pltpu.VMEM((PULSES, WIDTH), f32),
            pltpu.VMEM((STEPS, PULSES, WIDTH), bf16),
            dma((LAGS,)), dma, dma, dma,
            dma((SENT,)), dma((SENT,)), dma((SENT,)), dma((SENT,)),
            dma((SENT,)), dma((SENT,)), dma((SENT,)), dma((SENT,)), dma((SENT,)),
            dma((STEPS,)), dma((STEPS,)), dma((STEPS,)), dma,
        ],
        compiler_params=pltpu.CompilerParams(
            collective_id=0, has_side_effects=True, vmem_limit_bytes=60 << 20
        ),
    )(columns, counts, history, tiles, inverse, excitation)


def solution(mesh):
    return jax.shard_map(
        local,
        mesh=mesh,
        in_specs=(
            P("lag", None, None),
            P("lag", "row", None, None, None),
            P("lag", "row", None),
            P("lag", "row"),
            P("row", None, None),
            P(None, None, "row"),
        ),
        out_specs=P(None, None, "row"),
        check_vma=False,
    )
```

```python
import jax
import jax.numpy as jnp
from jax import lax
from jax.experimental import pallas as pl
from jax.experimental.pallas import tpu as pltpu
from jax.sharding import PartitionSpec as P

MESH = pl.DeviceIdType.MESH
LAG_AXIS, ROW_AXIS = "lag", "row"
NY, NZ, NX = 2, 4, 4
ROWS = NY * NZ * NX
GROUPS = 4
LAGS = 16
RB = 4
KS = 8
T = 128
PULSES = 16
HALF = 8
STEPS = 16
SENT = STEPS - 1
NB = 128
WIDTH = RB * T
NEAR = 8


def ring_hops(d, n):
    return min(d, n - d)


OFFSETS = sorted(
    [(a, b, c) for a in range(NY) for b in range(NZ) for c in range(NX)][1:],
    key=lambda o: -(o[0] + ring_hops(o[1], NZ) + ring_hops(o[2], NX)),
)


def dot_t(a, b):
    return lax.dot_general(a, b, (((1,), (1,)), ((), ())), preferred_element_type=jnp.float32)


def kernel(
    columns, counts, hist_hbm, tiles_hbm, inv_hbm, exc_hbm, out_ref,
    tiles, h0, land, work, inv, exc, acc, base, first_lag, part, parts, solf, outbuf,
    tsem, hsem, isem, esem, recv_a, recv_b, send_a, send_b,
    hrecv, slice_recv, slice_send, fwd_send, stream_send, part_send, part_recv, out_send, out_recv,
):
    g = lax.axis_index(LAG_AXIS)
    r = lax.axis_index(ROW_AXIS)
    y, z, x = r // (NZ * NX), (r // NX) % NZ, r % NX
    partner = (NY - 1 - y) * (NZ * NX) + z * NX + x

    def peer(o):
        return ((y + o[0]) % NY) * (NZ * NX) + ((z + o[1]) % NZ) * NX + (x + o[2]) % NX

    barrier = pltpu.get_barrier_semaphore()

    def greet(lag, row):
        pl.semaphore_signal(barrier, inc=1, device_id=(lag, row), device_id_type=MESH)

    @pl.when(g % 2 == 0)
    def _():
        for o in OFFSETS:
            greet(g, peer(o))

    @pl.when(g == 0)
    def _():
        for other in (1, 2, 3):
            greet(other, r)

    @pl.when(g == 1)
    def _():
        greet(0, r)
        greet(2, partner)

    @pl.when(g == 2)
    def _():
        greet(0, r)
        greet(3, r)
        greet(1, partner)

    @pl.when(g == 3)
    def _():
        greet(0, r)
        greet(2, r)

    def wait_for_greetings():
        @pl.when(g % 2 == 0)
        def _():
            pl.semaphore_wait(barrier, ROWS - 1 + 3)

        @pl.when(g % 2 == 1)
        def _():
            pl.semaphore_wait(barrier, 2)

    def load_block(c, carry):
        pltpu.make_async_copy(
            hist_hbm.at[:, :, pl.ds(pl.multiple_of(c * T, T), T)], h0.at[:, c], hsem
        ).start()
        return carry

    lax.fori_loop(0, NB, load_block, 0)
    for l in range(LAGS):
        pltpu.make_async_copy(tiles_hbm.at[l], tiles.at[l], tsem.at[l]).start()
    inv_copy = pltpu.make_async_copy(inv_hbm, inv, isem)
    inv_copy.start()
    exc_copy = pltpu.make_async_copy(exc_hbm, exc, esem)
    exc_copy.start()

    zero_block = jnp.zeros((T // 8, T), jnp.bfloat16)
    acc[...] = jnp.zeros_like(acc)
    for e in range(LAGS):
        h0[e, NB] = zero_block
    for tau in range(SENT):
        work[tau, 0, NB] = zero_block
        work[tau, 1, NB] = zero_block

    pltpu.make_async_copy(h0.at[:, pl.ds(0, NB)], h0.at[:, pl.ds(0, NB)], hsem).wait()

    def slice_copy(tau):
        cs = pl.ds(RB * partner, RB)
        return pltpu.make_async_remote_copy(
            h0.at[LAGS - 1 - tau, cs],
            land.at[tau, cs],
            slice_send.at[tau],
            slice_recv.at[tau],
            device_id=(2, partner),
            device_id_type=MESH,
        )

    def stream_copy(tau):
        return pltpu.make_async_remote_copy(
            h0.at[LAGS - 1 - tau, pl.ds(0, NB)],
            land.at[tau],
            stream_send.at[tau],
            hrecv.at[tau],
            device_id=(g + 1, r),
            device_id_type=MESH,
        )

    def send_history():
        @pl.when(g == 1)
        def _():
            def one(tau, carry):
                slice_copy(tau).start()
                return carry

            lax.fori_loop(0, SENT, one, 0)

        @pl.when(g % 2 == 0)
        def _():
            def one(tau, carry):
                stream_copy(tau).start()
                return carry

            lax.fori_loop(0, SENT, one, 0)

    def forward_copy(tau, o):
        here = land.at[tau, pl.ds(RB * r, RB)]
        return pltpu.make_async_remote_copy(
            here, here, fwd_send.at[tau], hrecv.at[tau], device_id=(2, peer(o)), device_id_type=MESH
        )

    def forward(tau):
        here = land.at[tau, pl.ds(RB * r, RB)]
        pltpu.make_async_copy(here, here, slice_recv.at[tau]).wait()
        for o in OFFSETS:
            forward_copy(tau, o).start()

    def column(l, b, k):
        return jnp.where(k < counts[b, l], columns[b, k, l], NB)

    def weights(l, b):
        return jnp.concatenate([tiles[l, b, k] for k in range(KS)], axis=1)

    for quarter in range(4):
        entries = 4 * quarter + 4

        def own_lag(l, carry):
            pltpu.make_async_copy(tiles.at[l], tiles.at[l], tsem.at[l]).wait()
            for b in range(RB):
                xs = [
                    h0[0:entries, column(l, b, k)].reshape(entries * PULSES, T) for k in range(KS)
                ]
                got = dot_t(jnp.concatenate(xs, axis=1), weights(l, b))
                here = (pl.ds(LAGS - 1 - l, entries), slice(None), pl.ds(b * T, T))
                acc[here] += got.reshape(entries, PULSES, T)
            return carry

        lax.fori_loop(4 * quarter, 4 * quarter + 4, own_lag, 0)
        if quarter == 0:
            wait_for_greetings()
            send_history()
        if quarter == 2:

            @pl.when(g == 2)
            def _():
                forward(0)


    inv_copy.wait()
    exc_copy.wait()

    def part_copy(s, ch):
        return pltpu.make_async_remote_copy(
            part.at[s, ch],
            parts.at[s, ch, g - 1],
            part_send.at[s],
            part_recv.at[s],
            device_id=(0, r),
            device_id_type=MESH,
        )

    def send_part(s):
        for ch in range(2):
            part[s, ch] = acc[STEPS - 1 - s, pl.ds(ch * HALF, HALF), :]
        for ch in range(2):
            part_copy(s, ch).start()

    @pl.when(g > 0)
    def _():
        send_part(0)

        def entry(tau, carry):
            @pl.when((g == 2) & (tau < SENT - 1))
            def _():
                forward(tau + 1)

            @pl.when(g == 2)
            def _():
                arrived = land.at[tau, pl.ds(0, NB - RB)]
                pltpu.make_async_copy(arrived, arrived, hrecv.at[tau]).wait()

            @pl.when(g != 2)
            def _():
                pltpu.make_async_copy(land.at[tau], land.at[tau], hrecv.at[tau]).wait()

            work[tau, 0, pl.ds(0, NB)] = land[tau]

            def push(lag, carry):
                for b in range(RB):
                    xs = [work[tau, 0, column(lag - 1, b, k)] for k in range(KS)]
                    got = dot_t(jnp.concatenate(xs, axis=1), weights(lag - 1, b))
                    here = (STEPS - 1 - (tau + lag), slice(None), pl.ds(b * T, T))
                    acc[here] += got
                return carry

            push(1, 0)
            send_part(tau + 1)
            lax.fori_loop(2, STEPS - tau, push, 0)
            return carry

        lax.fori_loop(0, SENT, entry, 0)

    low = lax.broadcasted_iota(jnp.int32, (2 * HALF, T), 0) < HALF
    keep_low = jnp.where(low, 1.0, 0.0).astype(jnp.bfloat16)
    keep_high = jnp.where(low, 0.0, 1.0).astype(jnp.bfloat16)
    recv = (recv_a, recv_b)
    send = (send_a, send_b)

    def own_slot(s, ch):
        return land.at[s, pl.ds(ch * (NB // 2) + 2 * r, 2)]

    def solution_copy(s, ch, o):
        here = own_slot(s, ch)
        return pltpu.make_async_remote_copy(
            here, here, send[ch].at[s], recv[ch].at[s], device_id=(0, peer(o)), device_id_type=MESH
        )

    def out_copy(s, other):
        return pltpu.make_async_remote_copy(
            outbuf.at[s], outbuf.at[s], out_send.at[s], out_recv, device_id=(other, r), device_id_type=MESH
        )

    def folded(got):
        return got[0:HALF] + got[HALF : 2 * HALF]

    def set_base(s):
        pltpu.make_async_copy(parts.at[s], parts.at[s], part_recv.at[s]).wait()
        other = [parts[s, ch, 0] + parts[s, ch, 1] + parts[s, ch, 2] for ch in range(2)]
        field = exc[s] - (acc[STEPS - 1 - s] + jnp.concatenate(other, axis=0))
        rhs = field.astype(jnp.bfloat16)
        for b in range(RB):
            base[:, pl.ds(b * T, T)] = dot_t(rhs[:, b * T : (b + 1) * T], inv[b])

    def chain(s, ch, first):
        if not first:
            tau = s - 1
            arrived = land.at[tau, pl.ds(0, NB // 2 - 2)]
            pltpu.make_async_copy(arrived, arrived, recv[ch].at[tau]).wait()
            pairs = land[tau, pl.ds(ch * (NB // 2), NB // 2)]
            split = jnp.stack([pairs * keep_low, pairs * keep_high], axis=1)
            work[tau, ch, pl.ds(0, NB)] = split.reshape(NB, 2 * HALF, T)
        solved = []
        for b in range(RB):
            cols = pl.ds(b * T, T)
            value = base[pl.ds(ch * HALF, HALF), cols]
            if not first:
                xs = [work[tau, ch, column(0, b, k)] for k in range(KS)]
                got = jnp.dot(
                    jnp.concatenate(xs, axis=1), first_lag[b], preferred_element_type=jnp.float32
                )
                value = value - folded(got)
            solved.append(value)
        for b in range(RB):
            solf[pl.ds(ch * HALF, HALF), pl.ds(b * T, T)] = solved[b]

        def publish():
            for i in range(2):
                pair = jnp.concatenate([solved[2 * i], solved[2 * i + 1]], axis=0)
                land[s, ch * (NB // 2) + 2 * r + i] = pair.astype(jnp.bfloat16)
            for o in OFFSETS:
                solution_copy(s, ch, o).start()

        if first:
            publish()
        else:
            pl.when(s < SENT)(publish)

    def hand_out(s):
        outbuf[s] = solf[...].astype(jnp.bfloat16)
        for other in (1, 2, 3):
            out_copy(s, other).start()

    def later(s):
        near = jnp.minimum(s, NEAR - 1)
        far = jnp.maximum(NEAR - s, 0)

        def one(n, carry):
            is_near = n < near
            lag = jnp.where(is_near, n + 2, n - near + NEAR + 1)
            tau = jnp.where(is_near, s + 1 - lag, s - 1)
            target = tau + lag
            for b in range(RB):
                cs = [column(lag - 1, b, k) for k in range(KS)]
                xa = jnp.concatenate([work[tau, 0, c] for c in cs], axis=1)
                xb = jnp.concatenate([work[tau, 1, c] for c in cs], axis=1)
                got = dot_t(jnp.concatenate([xa, xb], axis=0), weights(lag - 1, b))
                here = (STEPS - 1 - target, slice(None), pl.ds(b * T, T))
                acc[here] += jnp.concatenate(
                    [folded(got[0 : 2 * HALF]), folded(got[2 * HALF : 4 * HALF])], axis=0
                )
            return carry

        lax.fori_loop(0, near + far, one, 0)

    @pl.when(g == 0)
    def _():
        for b in range(RB):
            for k in range(KS):
                product = lax.dot_general(
                    tiles[0, b, k], inv[b], (((0,), (1,)), ((), ())), preferred_element_type=jnp.float32
                )
                first_lag[b, pl.ds(k * T, T), :] = product.astype(jnp.bfloat16)
        set_base(0)
        chain(0, 0, True)
        chain(0, 1, True)
        hand_out(0)
        set_base(1)

        def step(s, carry):
            chain(s, 0, False)
            chain(s, 1, False)
            hand_out(s)

            @pl.when(s < STEPS - 1)
            def _():
                later(s)
                set_base(s + 1)

            return carry

        lax.fori_loop(1, STEPS, step, 0)

        def drain(s, carry):
            sent = land.at[s, pl.ds(0, NB // 2 - 2)]
            for ch in range(2):
                pltpu.make_async_copy(sent, sent, send[ch].at[s]).wait()
            return carry

        lax.fori_loop(0, SENT, drain, 0)

        def drain_out(s, carry):
            for other in (1, 2, 3):
                out_copy(s, other).wait_send()
            return carry

        lax.fori_loop(0, STEPS, drain_out, 0)

    @pl.when(g > 0)
    def _():
        pltpu.make_async_copy(outbuf, outbuf, out_recv).wait()

        def drain(s, carry):
            pltpu.make_async_copy(part.at[s], part.at[s], part_send.at[s]).wait()
            return carry

        lax.fori_loop(0, STEPS, drain, 0)

    @pl.when(g % 2 == 0)
    def _():
        def drain(tau, carry):
            stream_copy(tau).wait_send()
            return carry

        lax.fori_loop(0, SENT, drain, 0)

    @pl.when(g == 1)
    def _():
        def drain(tau, carry):
            sent = land.at[tau, pl.ds(0, RB)]
            pltpu.make_async_copy(sent, sent, slice_send.at[tau]).wait()
            return carry

        lax.fori_loop(0, SENT, drain, 0)

    @pl.when(g == 2)
    def _():
        def drain(tau, carry):
            sent = land.at[tau, pl.ds(0, NB - RB)]
            pltpu.make_async_copy(sent, sent, fwd_send.at[tau]).wait()
            return carry

        lax.fori_loop(0, SENT, drain, 0)

    out_ref[...] = outbuf[...]


def local(history, tiles, columns, counts, inverse, excitation):
    smem = pl.BlockSpec(memory_space=pltpu.SMEM)
    hbm = pl.BlockSpec(memory_space=pl.ANY)
    dma = pltpu.SemaphoreType.DMA
    bf16, f32 = jnp.bfloat16, jnp.float32
    return pl.pallas_call(
        kernel,
        out_shape=jax.ShapeDtypeStruct((STEPS, PULSES, WIDTH), bf16),
        in_specs=[smem, smem, hbm, hbm, hbm, hbm],
        out_specs=pl.BlockSpec(memory_space=pltpu.VMEM),
        scratch_shapes=[
            pltpu.VMEM((LAGS, RB, KS, T, T), bf16),
            pltpu.VMEM((LAGS, NB + 1, PULSES, T), bf16),
            pltpu.VMEM((SENT, NB, PULSES, T), bf16),
            pltpu.VMEM((SENT, 2, NB + 1, PULSES, T), bf16),
            pltpu.VMEM((RB, T, T), bf16),
            pltpu.VMEM((STEPS, PULSES, WIDTH), f32),
            pltpu.VMEM((STEPS + 3, PULSES, WIDTH), f32),
            pltpu.VMEM((PULSES, WIDTH), f32),
            pltpu.VMEM((RB, KS * T, T), bf16),
            pltpu.VMEM((STEPS, 2, HALF, WIDTH), f32),
            pltpu.VMEM((STEPS, 2, 3, HALF, WIDTH), f32),
            pltpu.VMEM((PULSES, WIDTH), f32),
            pltpu.VMEM((STEPS, PULSES, WIDTH), bf16),
            dma((LAGS,)), dma, dma, dma,
            dma((SENT,)), dma((SENT,)), dma((SENT,)), dma((SENT,)),
            dma((SENT,)), dma((SENT,)), dma((SENT,)), dma((SENT,)), dma((SENT,)),
            dma((STEPS,)), dma((STEPS,)), dma((STEPS,)), dma,
        ],
        compiler_params=pltpu.CompilerParams(
            collective_id=0, has_side_effects=True, vmem_limit_bytes=60 << 20
        ),
    )(columns.transpose(1, 2, 0), counts.T, history, tiles, inverse, excitation)


def solution(mesh):
    return jax.shard_map(
        local,
        mesh=mesh,
        in_specs=(
            P("lag", None, None),
            P("lag", "row", None, None, None),
            P("lag", "row", None),
            P("lag", "row"),
            P("row", None, None),
            P(None, None, "row"),
        ),
        out_specs=P(None, None, "row"),
        check_vma=False,
    )
```

```python
import jax
import jax.numpy as jnp
from jax import lax
from jax.experimental import pallas as pl
from jax.experimental.pallas import tpu as pltpu
from jax.sharding import PartitionSpec as P

MESH = pl.DeviceIdType.MESH
LAG_AXIS, ROW_AXIS = "lag", "row"
NY, NZ, NX = 2, 4, 4
ROWS = NY * NZ * NX
GROUPS = 4
LAGS = 16
RB = 4
KS = 8
T = 128
PULSES = 16
HALF = 8
STEPS = 16
SENT = STEPS - 1
NB = 128
WIDTH = RB * T
EARLY = 3
AHEAD = 2
NEAR = 8
SPARE = STEPS - NEAR - 2


def ring_hops(d, n):
    return min(d, n - d)


OFFSETS = sorted(
    [(a, b, c) for a in range(NY) for b in range(NZ) for c in range(NX)][1:],
    key=lambda o: -(o[0] + ring_hops(o[1], NZ) + ring_hops(o[2], NX)),
)

EVERY = OFFSETS + [(0, 0, 0)]


def dot_t(a, b):
    return lax.dot_general(a, b, (((1,), (1,)), ((), ())), preferred_element_type=jnp.float32)


def kernel(
    columns, counts, hist_hbm, tiles_hbm, inv_hbm, exc_hbm, out_ref,
    tiles, h0, land, slices, work, inv, exc, acc, soon, base, first_lag, part, parts, solf, outbuf,
    tsem, hsem, isem, esem, recv_a, recv_b, send_a, send_b,
    hrecv, slice_recv, slice_send, fwd_send, stream_send, part_send, part_recv, out_send, out_recv,
):
    g = lax.axis_index(LAG_AXIS)
    r = lax.axis_index(ROW_AXIS)
    y, z, x = r // (NZ * NX), (r // NX) % NZ, r % NX
    partner = (NY - 1 - y) * (NZ * NX) + z * NX + x

    def peer(o):
        return ((y + o[0]) % NY) * (NZ * NX) + ((z + o[1]) % NZ) * NX + (x + o[2]) % NX

    barrier = pltpu.get_barrier_semaphore()

    def greet(lag, row):
        pl.semaphore_signal(barrier, inc=1, device_id=(lag, row), device_id_type=MESH)

    @pl.when(g == 0)
    def _():
        for o in OFFSETS:
            greet(0, peer(o))
        for other in (1, 2, 3):
            greet(other, r)

    @pl.when(g == 1)
    def _():
        greet(0, r)
        greet(3, partner)

    @pl.when(g == 2)
    def _():
        for o in EVERY:
            greet(3, peer(o))
        greet(0, r)

    @pl.when(g == 3)
    def _():
        for o in EVERY:
            greet(2, peer(o))
        greet(0, r)
        greet(1, partner)

    def wait_for_greetings():
        @pl.when(g % 2 == 0)
        def _():
            pl.semaphore_wait(barrier, jnp.where(g == 0, ROWS - 1 + 3, ROWS + 1))

        @pl.when(g % 2 == 1)
        def _():
            pl.semaphore_wait(barrier, jnp.where(g == 1, 2, ROWS + 2))

    def load_block(c, carry):
        pltpu.make_async_copy(
            hist_hbm.at[:, :, pl.ds(pl.multiple_of(c * T, T), T)], h0.at[:, c], hsem
        ).start()
        return carry

    lax.fori_loop(0, NB, load_block, 0)
    for l in range(LAGS):
        pltpu.make_async_copy(tiles_hbm.at[l], tiles.at[l], tsem.at[l]).start()
    inv_copy = pltpu.make_async_copy(inv_hbm, inv, isem)
    inv_copy.start()
    exc_copy = pltpu.make_async_copy(exc_hbm, exc, esem)
    exc_copy.start()

    zero_block = jnp.zeros((T // 8, T), jnp.bfloat16)
    acc[...] = jnp.zeros_like(acc)
    soon[...] = jnp.zeros_like(soon)
    for e in range(LAGS):
        h0[e, NB] = zero_block
    for tau in range(SENT):
        work[tau, 0, NB] = zero_block
        work[tau, 1, NB] = zero_block

    pltpu.make_async_copy(h0.at[:, pl.ds(0, NB)], h0.at[:, pl.ds(0, NB)], hsem).wait()

    def slice_copy(tau):
        cs = pl.ds(RB * partner, RB)
        return pltpu.make_async_remote_copy(
            h0.at[LAGS - 1 - tau, cs],
            slices.at[tau],
            slice_send.at[tau],
            slice_recv.at[tau],
            device_id=(3, partner),
            device_id_type=MESH,
        )

    def stream_copy(tau):
        return pltpu.make_async_remote_copy(
            h0.at[LAGS - 1 - tau, pl.ds(0, NB)],
            land.at[tau],
            stream_send.at[tau],
            hrecv.at[tau],
            device_id=(g + 1, r),
            device_id_type=MESH,
        )

    def send_history():
        @pl.when(g == 1)
        def _():
            def one(tau, carry):
                slice_copy(tau).start()
                return carry

            lax.fori_loop(0, SENT, one, 0)

        @pl.when(g % 2 == 0)
        def _():
            def one(tau, carry):
                stream_copy(tau).start()
                return carry

            lax.fori_loop(0, SENT, one, 0)

    def forward(tau):
        here = slices.at[tau]
        pltpu.make_async_copy(here, here, slice_recv.at[tau]).wait()
        for o in EVERY:
            pltpu.make_async_remote_copy(
                here,
                land.at[tau, pl.ds(RB * r, RB)],
                fwd_send.at[tau],
                hrecv.at[tau],
                device_id=(2, peer(o)),
                device_id_type=MESH,
            ).start()

    def column(l, b, k):
        return jnp.where(k < counts[b, l], columns[b, k, l], NB)

    def weights(l, b):
        return jnp.concatenate([tiles[l, b, k] for k in range(KS)], axis=1)

    def row_of(s):
        return SPARE + STEPS - 1 - s

    def meet_own(l, first, entries, total, start):
        for b in range(RB):
            xs = [
                h0[pl.ds(first, entries), column(l, b, k)].reshape(entries * PULSES, T)
                for k in range(KS)
            ]
            got = dot_t(jnp.concatenate(xs, axis=1), weights(l, b))
            here = (pl.ds(start, entries), slice(None), pl.ds(b * T, T))
            total[here] += got.reshape(entries, PULSES, T)

    def first_steps(l, carry):
        pltpu.make_async_copy(tiles.at[l], tiles.at[l], tsem.at[l]).wait()
        meet_own(l, l - 1, 2, soon, 0)
        return carry

    def quarter_of_lags(quarter):
        entries = 4 * quarter + 4

        def own_lag(l, carry):
            meet_own(l, 0, entries, acc, SPARE + LAGS - 1 - l)
            return carry

        lax.fori_loop(4 * quarter, 4 * quarter + 4, own_lag, 0)

    pltpu.make_async_copy(tiles.at[0], tiles.at[0], tsem.at[0]).wait()
    meet_own(0, 0, 1, soon, 1)
    lax.fori_loop(1, LAGS // 2, first_steps, 0)
    wait_for_greetings()
    send_history()
    lax.fori_loop(LAGS // 2, 12, first_steps, 0)
    @pl.when(g == 3)
    def _():
        for tau in range(1):
            forward(tau)

    lax.fori_loop(12, LAGS, first_steps, 0)
    inv_copy.wait()
    exc_copy.wait()

    def part_copy(s, ch):
        return pltpu.make_async_remote_copy(
            part.at[s, ch],
            parts.at[s, ch, g - 1],
            part_send.at[s],
            part_recv.at[s],
            device_id=(0, r),
            device_id_type=MESH,
        )

    def send_part(s):
        total, row = (soon, 1 - s) if isinstance(s, int) else (acc, row_of(s))
        for ch in range(2):
            part[s, ch] = total[row, pl.ds(ch * HALF, HALF), :]
        for ch in range(2):
            part_copy(s, ch).start()

    @pl.when(g > 0)
    def _():
        send_part(0)

        @pl.when(g == 3)
        def _():
            for tau in range(1, AHEAD):
                forward(tau)

        def meet(lag, first, entries, total, start):
            for b in range(RB):
                xs = [
                    work[pl.ds(first, entries), 0, column(lag - 1, b, k)].reshape(entries * PULSES, T)
                    for k in range(KS)
                ]
                got = dot_t(jnp.concatenate(xs, axis=1), weights(lag - 1, b))
                here = (pl.ds(start, entries), slice(None), pl.ds(b * T, T))
                total[here] += got.reshape(entries, PULSES, T)

        def meet_later(lag, first, entries):
            meet(lag, first, entries, acc, SPARE + 1 - lag + first)

        def arrive(tau):
            pltpu.make_async_copy(land.at[tau], land.at[tau], hrecv.at[tau]).wait()
            work[SENT - 1 - tau, 0, pl.ds(0, NB)] = land[tau]

        def go_on(tau):
            @pl.when((g == 3) & (tau < SENT - AHEAD))
            def _():
                forward(tau + AHEAD)

            def near(lag, carry):
                meet_later(lag, SENT - 1 - (tau + 2 - lag), 1)
                return carry

            @pl.when(tau < SENT - 1)
            def _():
                lax.fori_loop(2, jnp.minimum(NEAR, tau + 2) + 1, near, 0)

            @pl.when((tau >= NEAR - 1) & (tau < SENT - 1))
            def _():
                meet_later(tau + 2, NEAR, SENT - NEAR)

        for quarter in range(EARLY):
            quarter_of_lags(quarter)
        arrive(0)
        meet(1, SENT - 1, 1, soon, 0)
        send_part(1)
        for quarter in range(EARLY, 4):
            quarter_of_lags(quarter)
        go_on(jnp.int32(0))

        def entry(tau, carry):
            arrive(tau)
            meet_later(1, SENT - 1 - tau, 1)
            send_part(tau + 1)
            go_on(tau)
            return carry

        lax.fori_loop(1, SENT, entry, 0)

    low = lax.broadcasted_iota(jnp.int32, (2 * HALF, T), 0) < HALF
    keep_low = jnp.where(low, 1.0, 0.0).astype(jnp.bfloat16)
    keep_high = jnp.where(low, 0.0, 1.0).astype(jnp.bfloat16)
    recv = (recv_a, recv_b)
    send = (send_a, send_b)

    def own_slot(s, ch):
        return land.at[s, pl.ds(ch * (NB // 2) + 2 * r, 2)]

    def solution_copy(s, ch, o):
        here = own_slot(s, ch)
        return pltpu.make_async_remote_copy(
            here, here, send[ch].at[s], recv[ch].at[s], device_id=(0, peer(o)), device_id_type=MESH
        )

    def out_copy(s, other):
        return pltpu.make_async_remote_copy(
            outbuf.at[s], outbuf.at[s], out_send.at[s], out_recv, device_id=(other, r), device_id_type=MESH
        )

    def folded(got):
        return got[0:HALF] + got[HALF : 2 * HALF]

    def set_base(s):
        pltpu.make_async_copy(parts.at[s], parts.at[s], part_recv.at[s]).wait()
        other = [parts[s, ch, 0] + parts[s, ch, 1] + parts[s, ch, 2] for ch in range(2)]
        own = soon[1 - s] if isinstance(s, int) else acc[row_of(s)]
        field = exc[s] - (own + jnp.concatenate(other, axis=0))
        high = field.astype(jnp.bfloat16)
        rest = (field - high.astype(jnp.float32)).astype(jnp.bfloat16)
        rhs = jnp.concatenate([high, rest], axis=0)
        for b in range(RB):
            got = dot_t(rhs[:, b * T : (b + 1) * T], inv[b])
            base[:, pl.ds(b * T, T)] = got[0:PULSES] + got[PULSES : 2 * PULSES]

    def chain(s, ch, first):
        if not first:
            tau = s - 1
            arrived = land.at[tau, pl.ds(0, NB // 2 - 2)]
            pltpu.make_async_copy(arrived, arrived, recv[ch].at[tau]).wait()
            pairs = land[tau, pl.ds(ch * (NB // 2), NB // 2)]
            split = jnp.stack([pairs * keep_low, pairs * keep_high], axis=1)
            work[tau, ch, pl.ds(0, NB)] = split.reshape(NB, 2 * HALF, T)
        solved = []
        for b in range(RB):
            cols = pl.ds(b * T, T)
            value = base[pl.ds(ch * HALF, HALF), cols]
            if not first:
                xs = [work[tau, ch, column(0, b, k)] for k in range(KS)]
                got = jnp.dot(
                    jnp.concatenate(xs, axis=1), first_lag[b], preferred_element_type=jnp.float32
                )
                value = value - folded(got)
            solved.append(value)
        for b in range(RB):
            solf[pl.ds(ch * HALF, HALF), pl.ds(b * T, T)] = solved[b]

        def publish():
            for i in range(2):
                pair = jnp.concatenate([solved[2 * i], solved[2 * i + 1]], axis=0)
                land[s, ch * (NB // 2) + 2 * r + i] = pair.astype(jnp.bfloat16)
            for o in OFFSETS:
                solution_copy(s, ch, o).start()

        if first:
            publish()
        else:
            pl.when(s < SENT)(publish)

    def hand_out(s):
        outbuf[s] = solf[...].astype(jnp.bfloat16)
        for other in (1, 2, 3):
            out_copy(s, other).start()

    def later(s):
        near = jnp.minimum(s, NEAR - 1)
        far = jnp.maximum(NEAR - s, 0)

        def one(n, carry):
            is_near = n < near
            lag = jnp.where(is_near, n + 2, n - near + NEAR + 1)
            tau = jnp.where(is_near, s + 1 - lag, s - 1)
            target = tau + lag
            for b in range(RB):
                cs = [column(lag - 1, b, k) for k in range(KS)]
                xa = jnp.concatenate([work[tau, 0, c] for c in cs], axis=1)
                xb = jnp.concatenate([work[tau, 1, c] for c in cs], axis=1)
                got = dot_t(jnp.concatenate([xa, xb], axis=0), weights(lag - 1, b))
                here = (row_of(target), slice(None), pl.ds(b * T, T))
                acc[here] += jnp.concatenate(
                    [folded(got[0 : 2 * HALF]), folded(got[2 * HALF : 4 * HALF])], axis=0
                )
            return carry

        lax.fori_loop(0, near + far, one, 0)

    @pl.when(g == 0)
    def _():
        for b in range(RB):
            for k in range(KS):
                product = lax.dot_general(
                    tiles[0, b, k], inv[b], (((0,), (1,)), ((), ())), preferred_element_type=jnp.float32
                )
                first_lag[b, pl.ds(k * T, T), :] = product.astype(jnp.bfloat16)
        quarter_of_lags(0)
        quarter_of_lags(1)
        set_base(0)
        chain(0, 0, True)
        chain(0, 1, True)
        quarter_of_lags(2)
        quarter_of_lags(3)
        hand_out(0)
        set_base(1)

        def step(s, carry):
            chain(s, 0, False)
            chain(s, 1, False)
            hand_out(s)

            @pl.when(s < STEPS - 1)
            def _():
                later(s)
                set_base(s + 1)

            return carry

        lax.fori_loop(1, STEPS, step, 0)

        def drain(s, carry):
            sent = land.at[s, pl.ds(0, NB // 2 - 2)]
            for ch in range(2):
                pltpu.make_async_copy(sent, sent, send[ch].at[s]).wait()
            return carry

        lax.fori_loop(0, SENT, drain, 0)

        def drain_out(s, carry):
            for other in (1, 2, 3):
                out_copy(s, other).wait_send()
            return carry

        lax.fori_loop(0, STEPS, drain_out, 0)

    @pl.when(g > 0)
    def _():
        pltpu.make_async_copy(outbuf, outbuf, out_recv).wait()

        def drain(s, carry):
            pltpu.make_async_copy(part.at[s], part.at[s], part_send.at[s]).wait()
            return carry

        lax.fori_loop(0, STEPS, drain, 0)

    @pl.when(g % 2 == 0)
    def _():
        def drain(tau, carry):
            stream_copy(tau).wait_send()
            return carry

        lax.fori_loop(0, SENT, drain, 0)

    @pl.when(g == 1)
    def _():
        def drain(tau, carry):
            sent = land.at[tau, pl.ds(0, RB)]
            pltpu.make_async_copy(sent, sent, slice_send.at[tau]).wait()
            return carry

        lax.fori_loop(0, SENT, drain, 0)

    @pl.when(g == 3)
    def _():
        def drain(tau, carry):
            pltpu.make_async_copy(land.at[tau], land.at[tau], fwd_send.at[tau]).wait()
            return carry

        lax.fori_loop(0, SENT, drain, 0)

    out_ref[...] = outbuf[...]


def local(history, tiles, columns, counts, inverse, excitation):
    smem = pl.BlockSpec(memory_space=pltpu.SMEM)
    hbm = pl.BlockSpec(memory_space=pl.ANY)
    dma = pltpu.SemaphoreType.DMA
    bf16, f32 = jnp.bfloat16, jnp.float32
    return pl.pallas_call(
        kernel,
        out_shape=jax.ShapeDtypeStruct((STEPS, PULSES, WIDTH), bf16),
        in_specs=[smem, smem, hbm, hbm, hbm, hbm],
        out_specs=pl.BlockSpec(memory_space=pltpu.VMEM),
        scratch_shapes=[
            pltpu.VMEM((LAGS, RB, KS, T, T), bf16),
            pltpu.VMEM((LAGS, NB + 1, PULSES, T), bf16),
            pltpu.VMEM((SENT, NB, PULSES, T), bf16),
            pltpu.VMEM((SENT, RB, PULSES, T), bf16),
            pltpu.VMEM((SENT, 2, NB + 1, PULSES, T), bf16),
            pltpu.VMEM((RB, T, T), bf16),
            pltpu.VMEM((STEPS, PULSES, WIDTH), f32),
            pltpu.VMEM((SPARE + STEPS + 3, PULSES, WIDTH), f32),
            pltpu.VMEM((2, PULSES, WIDTH), f32),
            pltpu.VMEM((PULSES, WIDTH), f32),
            pltpu.VMEM((RB, KS * T, T), bf16),
            pltpu.VMEM((STEPS, 2, HALF, WIDTH), f32),
            pltpu.VMEM((STEPS, 2, 3, HALF, WIDTH), f32),
            pltpu.VMEM((PULSES, WIDTH), f32),
            pltpu.VMEM((STEPS, PULSES, WIDTH), bf16),
            dma((LAGS,)), dma, dma, dma,
            dma((SENT,)), dma((SENT,)), dma((SENT,)), dma((SENT,)),
            dma((SENT,)), dma((SENT,)), dma((SENT,)), dma((SENT,)), dma((SENT,)),
            dma((STEPS,)), dma((STEPS,)), dma((STEPS,)), dma,
        ],
        compiler_params=pltpu.CompilerParams(
            collective_id=0, has_side_effects=True, vmem_limit_bytes=60 << 20
        ),
    )(columns.transpose(1, 2, 0), counts.T, history, tiles, inverse, excitation)


def solution(mesh):
    return jax.shard_map(
        local,
        mesh=mesh,
        in_specs=(
            P("lag", None, None),
            P("lag", "row", None, None, None),
            P("lag", "row", None),
            P("lag", "row"),
            P("row", None, None),
            P(None, None, "row"),
        ),
        out_specs=P(None, None, "row"),
        check_vma=False,
    )
```
